32 devices in a mesh: groups: 2 (over x), pool: 16 (over z, y, core).
Axes of the slice: x: 2, y: 2, z: 4, core: 2. Of those that a mesh axis runs over, the one named last changes fastest.
Arguments:
- queries: bfloat16 [8192, 4096], P(('groups', 'pool')), parts along dimension 0, may hold values from -180 to 180
- new_kv: bfloat16 [8192, 1024], P(('groups', 'pool')), parts along dimension 0, may hold values from -6 to 6
- prefix_store: bfloat16 [2048, 8, 1024], P(('groups', 'pool')), parts along dimension 0, may hold values from -6 to 6
- page_owner: int32 [32, 16], P('groups'), parts along dimension 0, may hold values from 0 to 15, each once within a row
- page_slot: int32 [32, 16], P('groups'), parts along dimension 0, may hold values from 0 to 63
- prefix_pages: int32 [32], P('groups'), parts along dimension 0, may hold values from 1 to 16, 128 in all
- decode_dest: int32 [32, 32], P(('groups', 'pool')), parts along dimension 0, may hold values from 0 to 15, as said below
Outputs:
- attention: bfloat16 [8192, 4096], P(('groups', 'pool')), parts along dimension 0
- decode_inbox: bfloat16 [1024, 8, 1024], P(('groups', 'pool')), parts along dimension 0
The draws below stay inside these ranges and needn't reach their ends.
There are 2 independent parts, one for each index of `groups`. The reference program is written for one: setup_inputs(seed, part) draws one part's arguments, and reference() takes and returns one part's arrays. A program takes and returns all parts, laid end to end along the dimension named above; each array names one. Nothing has to cross between parts.
Inputs may be any that keep to these rules, and one draw needn't show every extreme that they name: `page_owner`: each row names every device of the pool once. `prefix_pages`: the entries sum to 128; the largest is 16. `decode_dest`: a device sends at most 2 of its 32 new pages to one decode owner; one decode owner receives exactly 2 from every device.
All inputs are finite; a program needn't handle non-finite values.
Results may differ from the reference program's by a relative error of at most 0.0027.
Values may be sent and summed in bfloat16 or wider, within the bound.
A program may use at most 128 MiB of HBM per device.

```python
import math
import jax
import jax.numpy as jnp
import numpy as np
from jax import lax

H = 32
KVH = 4
HD = 128
PAGE = 8
TOK_DEV = 256
PG_DEV = 64
KVW = 1024
MAXP = 16
TOTALP = 128
NEWP = 32
DMOST = 2
TOKENS = 4096
PAGES = 1024
INBOX = 512
N_POOL = 16


def kv_normal(key):
    return jnp.clip(jax.random.normal(jax.random.fold_in(key, 101), (TOKENS, KVW), jnp.float32), -6.0, 6.0)


def draw_new_kv(key, part):
    base = kv_normal(key)
    return base.astype(jnp.bfloat16)


def draw_queries(key, part):
    key = jax.random.fold_in(key, 3)
    drawn = 2.5 * jnp.clip(jax.random.normal(key, (TOKENS, H * HD), jnp.float32), -6.0, 6.0)
    return drawn.astype(jnp.bfloat16)


def draw_decode_dest(key, part):
    key = jax.random.fold_in(key, 5)
    pick_key, order_key = jax.random.split(key)
    special = jax.random.randint(pick_key, (), 0, N_POOL).astype(jnp.int32)
    candidates = jnp.arange((N_POOL - 1) * DMOST, dtype=jnp.int32) // DMOST

    def one_row(row_key):
        first_key, second_key = jax.random.split(row_key)
        others = jax.random.permutation(first_key, candidates)[:NEWP - DMOST]
        others = others + (others >= special).astype(jnp.int32)
        dest_row = jnp.concatenate([jnp.full((DMOST,), special, jnp.int32), others])
        return jax.random.permutation(second_key, dest_row)
    return jax.vmap(one_row)(jax.random.split(order_key, N_POOL)).astype(jnp.int32)


def place_ends(values, rng, low, top_value):
    dims = values.shape
    place = [jax.random.randint(jax.random.fold_in(rng, axis), (), 0, dims[axis]) for axis in range(len(dims))]
    values = values.at[tuple(place)].set(low)
    longest = dims.index(max(dims))
    place[longest] = (place[longest] + 1) % dims[longest]
    return values.at[tuple(place)].set(top_value)


def level_of(stream_key, dims, pieces, smallest, largest):
    factor_of, own = 1.0, jax.random.fold_in(stream_key, 6)
    for dim, blocks in pieces:
        draws = jnp.exp(jax.random.uniform(jax.random.fold_in(own, dim), (blocks,), jnp.float32, smallest / len(pieces), largest / len(pieces)))
        factor_of = factor_of * jnp.repeat(draws, dims[dim] // blocks).reshape([-1 if axis == dim else 1 for axis in range(len(dims))])
    return factor_of


def split_up(count, total, limit, slope):
    loads = [(1 << 20) // math.isqrt(standing ** slope) + 1 for standing in range(2, count + 1)]
    spare, counts = total - limit - (count - 1), [1] * (count - 1)
    while spare > 0:
        movable = [i for i in range(count - 1) if counts[i] < limit]
        mass, left = sum([loads[i] for i in movable]), spare
        for i in movable:
            extra = min(limit - counts[i], max(1, left * loads[i] // mass), spare)
            counts[i] = counts[i] + extra
            spare = spare - extra
    return np.array([limit] + counts)


def uneven(stream_key, number_of, total, reach, lean):
    if number_of == 2:
        one = jax.random.randint(stream_key, (), max(1, total - reach), min(reach, total - 1) + 1)
        return jnp.stack([one, total - one])
    tallies = jnp.asarray(split_up(number_of, total, reach, lean), jnp.int32)
    couples = (number_of - 1) // 2
    donor, receiver = tallies[1:1 + 2 * couples:2], tallies[2:2 + 2 * couples:2]
    room = jnp.minimum(donor - 1, reach - receiver)
    shifted = jax.random.randint(jax.random.fold_in(stream_key, 1), (couples,), 0, 1 << 20) % (room + 1)
    tallies = tallies.at[1:1 + 2 * couples:2].set(donor - shifted).at[2:2 + 2 * couples:2].set(receiver + shifted)
    return tallies[jax.random.permutation(jax.random.fold_in(stream_key, 2), number_of)]


def gaussian(stream_key, shape, scale, reach, cuts=(), held_as=jnp.bfloat16):
    values = jax.random.normal(stream_key, shape, jnp.float32) * scale
    if len(cuts) > 0:
        values = level_of(stream_key, shape, cuts, -0.22, 0.18) * values
    return jnp.clip(values, min=-reach, max=reach).astype(held_as)


def setup_inputs(seed: int = 0, part: int = 0) -> dict:
    arg_keys = jax.random.split(jax.random.key(seed), 8)
    own_keys = jax.random.split(jax.random.fold_in(arg_keys[7], part), 8)
    queries = draw_queries(jax.random.fold_in(jax.random.fold_in(arg_keys[7], part), 71), part)
    new_kv = draw_new_kv(jax.random.fold_in(jax.random.fold_in(arg_keys[7], part), 71), part)
    prefix_store = gaussian(own_keys[2], (PAGES, PAGE, KVW), 1.0, 6.0, ((0, 16),))
    page_owner = jax.vmap(lambda own: jax.random.permutation(own, N_POOL))(jax.random.split(own_keys[3], N_POOL)).reshape((N_POOL, MAXP)).astype(jnp.int32)
    page_slot = place_ends(jax.random.randint(own_keys[4], (N_POOL, MAXP), 0, PG_DEV), jax.random.fold_in(own_keys[4], 1), 0, PG_DEV - 1).astype(jnp.int32)
    prefix_pages = uneven(own_keys[5], N_POOL, TOTALP, MAXP, 2).astype(jnp.int32)
    decode_dest = draw_decode_dest(jax.random.fold_in(jax.random.fold_in(arg_keys[7], part), 71), part)
    return {"queries": queries, "new_kv": new_kv, "prefix_store": prefix_store, "page_owner": page_owner, "page_slot": page_slot, "prefix_pages": prefix_pages, "decode_dest": decode_dest}


masked_score = -1e+30

def reference(queries, new_kv, prefix_store, page_owner, page_slot, prefix_pages, decode_dest):
    group_size = H // KVH
    width_keys = KVH * HD
    prefix_tokens = N_POOL * PAGE
    token_ids = jnp.arange(TOK_DEV, dtype=jnp.int32)
    causal = token_ids[None, :] <= token_ids[:, None]
    page_of_key = jnp.arange(prefix_tokens, dtype=jnp.int32) // PAGE

    def one_device(device):
        page_rows = page_owner[device] * PG_DEV + page_slot[device]
        prefix_rows = prefix_store[page_rows].reshape(prefix_tokens, KVW)
        own_rows = lax.dynamic_slice_in_dim(new_kv, device * TOK_DEV, TOK_DEV, 0)
        query_rows = lax.dynamic_slice_in_dim(queries, device * TOK_DEV, TOK_DEV, 0)
        all_rows = jnp.concatenate([prefix_rows, own_rows], axis=0).astype(jnp.float32)
        key_rows = all_rows[:, :width_keys].reshape(-1, KVH, HD)
        value_rows = all_rows[:, width_keys:].reshape(-1, KVH, HD)
        grouped = query_rows.astype(jnp.float32).reshape(TOK_DEV, KVH, group_size, HD)
        scores = jnp.einsum('tkgd,skd->kgts', grouped, key_rows) * (1.0 / math.sqrt(HD))
        prefix_valid = jnp.broadcast_to((page_of_key < prefix_pages[device])[None, :], (TOK_DEV, prefix_tokens))
        key_valid = jnp.concatenate([prefix_valid, causal], axis=1)
        scores = jnp.where(key_valid, scores, masked_score)
        row_max = lax.optimization_barrier(jnp.max(scores, axis=-1, keepdims=True))
        weights = jnp.where(key_valid, jnp.exp(scores - row_max), 0.0)
        row_total = lax.optimization_barrier(jnp.sum(weights, axis=-1))
        rounded_weights = lax.optimization_barrier(weights.astype(jnp.bfloat16)).astype(jnp.float32)
        mixed_heads = jnp.einsum('kgts,skd->kgtd', rounded_weights, value_rows)
        mixed_heads = mixed_heads / row_total[..., None]
        return jnp.transpose(mixed_heads, (2, 0, 1, 3)).reshape(TOK_DEV, H * HD).astype(jnp.bfloat16)
    attention = lax.map(one_device, jnp.arange(N_POOL, dtype=jnp.int32)).reshape(TOKENS, H * HD)
    order_ids = jnp.arange(NEWP, dtype=jnp.int32)
    earlier = order_ids[None, :] < order_ids[:, None]
    same_owner = decode_dest[:, :, None] == decode_dest[:, None, :]
    rank_in_owner = lax.optimization_barrier(jnp.sum(same_owner & earlier[None, :, :], axis=-1)).astype(jnp.int32)
    senders = jnp.arange(N_POOL, dtype=jnp.int32)[:, None]
    position = (decode_dest * N_POOL + senders) * DMOST + rank_in_owner
    page_data = new_kv.reshape(N_POOL * NEWP, PAGE, KVW)
    decode_inbox = jnp.zeros((INBOX, PAGE, KVW), new_kv.dtype).at[position.reshape(-1).astype(jnp.int32)].set(page_data)
    return (attention, decode_inbox)
```

```python
import functools
import math

import jax
import jax.numpy as jnp
from jax import lax
from jax.experimental import pallas as pl
from jax.experimental.pallas import tpu as pltpu
from jax.sharding import PartitionSpec as P

HD = 128
PAGE = 8
KVH = 4
MASKED = -1e30
MESH = pl.DeviceIdType.MESH


def dot(a, b):
    return jnp.dot(a, b, preferred_element_type=jnp.float32)


def dot_t(a, b):
    return lax.dot_general(a, b, (((1,), (1,)), ((), ())), preferred_element_type=jnp.float32)


def iota(shape, dim):
    return lax.broadcasted_iota(jnp.int32, shape, dim)


def kernel(
    n, slots,
    q_hbm, kv_hbm, store_hbm, owner_ref, slot_ref, pages_ref, dest_ref,
    attn_hbm, inbox_hbm,
    q_ref, keys_ref, store_ref, pout_ref, arrived_ref, outbox_ref, bias_ref, attn_ref,
    in_sem, attn_sem, own_sem, psend, precv, isend, irecv,
):
    me = lax.axis_index("pool")
    tokens, width = q_ref.shape
    prefix = n * PAGE
    half = tokens // 2
    group = width // HD // KVH
    new_pages = dest_ref.shape[1]
    kv_width = keys_ref.shape[1]

    load_store = pltpu.make_async_copy(store_hbm, store_ref, in_sem.at[0])
    load_kv = pltpu.make_async_copy(kv_hbm, keys_ref.at[pl.ds(prefix, tokens)], in_sem.at[1])
    load_q = pltpu.make_async_copy(q_hbm, q_ref, in_sem.at[2])
    load_store.start()
    load_kv.start()
    load_q.start()

    def partner(i):
        step = n // 2 + ((i + 1) // 2) * (1 - 2 * (i % 2))
        return (me + step) % n

    barrier = pltpu.get_barrier_semaphore()

    def greet(i, carry):
        pl.semaphore_signal(barrier, inc=1, device_id={"pool": partner(i)}, device_id_type=MESH)
        return carry

    lax.fori_loop(0, n - 1, greet, 0)

    owner = owner_ref[...]
    pages_row = jnp.broadcast_to(pages_ref[...], (n, n))
    row_id, col_id = iota((n, n), 0), iota((n, n), 1)
    pages_col = jnp.sum(jnp.where(row_id == col_id, pages_row, 0), axis=1, keepdims=True)
    wanted = (owner == me) & (col_id < pages_col)
    slot_of = jnp.sum(jnp.where(wanted, slot_ref[...] + 1, 0), axis=1, keepdims=True) - 1
    expand = (iota((prefix, n), 0) // PAGE == iota((prefix, n), 1)).astype(jnp.bfloat16)
    slot_tok = dot(expand, jnp.broadcast_to(slot_of, (n, HD)).astype(jnp.float32).astype(jnp.bfloat16))
    stored_rows = store_ref.shape[0] * PAGE
    row_of = slot_tok.astype(jnp.int32) * PAGE + iota((prefix, HD), 0) % PAGE
    pick = jnp.concatenate(
        [(row_of == iota((prefix, HD), 1) + b).astype(jnp.float32).astype(jnp.bfloat16) for b in range(0, stored_rows, HD)],
        axis=1,
    )
    load_store.wait()
    stored = store_ref[...].astype(jnp.float32).reshape(stored_rows, kv_width).astype(jnp.bfloat16)
    pout_ref[...] = dot(pick, stored).reshape(n, PAGE, kv_width).astype(jnp.bfloat16)

    pl.semaphore_wait(barrier, n - 1)

    def send_page(i, carry):
        to = partner(i)
        pltpu.make_async_remote_copy(
            pout_ref.at[to], arrived_ref.at[me], psend, precv, device_id={"pool": to}, device_id_type=MESH
        ).start()
        return carry

    lax.fori_loop(0, n - 1, send_page, 0)

    dest = jnp.broadcast_to(dest_ref[...], (new_pages, new_pages))
    first, second = iota(dest.shape, 0), iota(dest.shape, 1)
    dest_col = jnp.sum(jnp.where(first == second, dest, 0), axis=1, keepdims=True)
    rank = jnp.sum(jnp.where((dest_col == dest) & (first < second), 1, 0), axis=0, keepdims=True)
    place = (dest_ref[...] * slots + rank).astype(jnp.float32)
    widen = (iota((new_pages, tokens), 1) // PAGE == iota((new_pages, tokens), 0)).astype(jnp.bfloat16)
    place_tok = dot(jnp.broadcast_to(place, (PAGE, new_pages)).astype(jnp.bfloat16), widen)[:1].astype(jnp.int32)
    out_rows = n * slots * PAGE
    goal = place_tok * PAGE + iota((1, tokens), 1) % PAGE
    permute = (iota((out_rows, tokens), 0) == goal).astype(jnp.float32).astype(jnp.bfloat16)
    load_kv.wait()
    new_rows = keys_ref[pl.ds(prefix, tokens), :]
    outbox_ref[...] = dot(permute, new_rows).reshape(n * slots, PAGE, kv_width).astype(jnp.bfloat16)

    def send_new(i, carry):
        to = partner(i)
        pltpu.make_async_remote_copy(
            outbox_ref.at[pl.ds(to * slots, slots)],
            inbox_hbm.at[pl.ds(me * slots, slots)],
            isend, irecv, device_id={"pool": to}, device_id_type=MESH,
        ).start()
        return carry

    lax.fori_loop(0, n - 1, send_new, 0)
    own_copy = pltpu.make_async_copy(
        outbox_ref.at[pl.ds(me * slots, slots)], inbox_hbm.at[pl.ds(me * slots, slots)], own_sem
    )
    own_copy.start()
    arrived_ref[me] = pout_ref[me]

    my_owner = owner_ref[pl.ds(me, 1), :]
    lane = iota((1, n), 1)
    my_pages = jnp.sum(jnp.where(lane == me, pages_ref[...], 0), axis=1, keepdims=True)
    held = jnp.broadcast_to(jnp.where(lane < my_pages, my_owner, -1), (n, n)) == row_id
    valid = jnp.sum(jnp.where(held, 1.0, 0.0), axis=1, keepdims=True)
    valid_tok = dot(expand, jnp.broadcast_to(valid, (n, half)).astype(jnp.bfloat16))
    bias_ref[pl.ds(0, prefix), :] = jnp.where(valid_tok > 0.5, 0.0, MASKED).astype(jnp.bfloat16)
    diagonal = jnp.where(iota((half, half), 0) > iota((half, half), 1), MASKED, 0.0).astype(jnp.bfloat16)
    bias_ref[pl.ds(prefix, half), :] = diagonal
    bias_ref[pl.ds(prefix + half, half), :] = jnp.zeros((half, half), jnp.bfloat16)
    bias_ref[pl.ds(prefix + 2 * half, half), :] = diagonal

    load_q.wait()
    pltpu.make_async_copy(
        arrived_ref.at[pl.ds(0, n - 1)], arrived_ref.at[pl.ds(0, n - 1)], precv
    ).wait()
    keys_ref[pl.ds(0, prefix), :] = (
        arrived_ref[...].astype(jnp.float32).reshape(prefix, kv_width).astype(jnp.bfloat16)
    )

    stack = group if prefix <= 256 else 1
    scale = math.log2(math.e) / math.sqrt(HD)
    unit = (iota((half, half), 0) == iota((half, half), 1)).astype(jnp.float32).astype(jnp.bfloat16)

    def attend(step, carry):
        kv_head = step * stack // group
        key_cols = pl.ds(pl.multiple_of(kv_head * HD, HD), HD)
        value_cols = pl.ds(pl.multiple_of(kv_head * HD + KVH * HD, HD), HD)
        heads = [pl.ds(pl.multiple_of((step * stack + i) * HD, HD), HD) for i in range(stack)]
        for part in range(2):
            rows = pl.ds(part * half, half)
            count = prefix + (part + 1) * half
            keys = keys_ref[pl.ds(0, count), key_cols]
            values = keys_ref[pl.ds(0, count), value_cols]
            bias = bias_ref[pl.ds(0, count), :] if part == 0 else jnp.concatenate(
                [bias_ref[pl.ds(0, prefix), :], bias_ref[pl.ds(prefix + half, 2 * half), :]], axis=0
            )
            keyed = jnp.concatenate([keys, bias], axis=1)
            summed = jnp.concatenate([values, jnp.ones((count, HD), jnp.bfloat16)], axis=1)
            query = jnp.concatenate(
                [jnp.concatenate([q_ref[rows, cols], unit], axis=1) for cols in heads], axis=0
            )
            scores = dot_t(query, keyed)
            top = jnp.max(scores, axis=1, keepdims=True)
            weights = jnp.exp2((scores - top) * scale).astype(jnp.bfloat16)
            mixed = dot(weights, summed)
            result = (mixed[:, :HD] / mixed[:, HD:]).astype(jnp.bfloat16)
            for i, cols in enumerate(heads):
                attn_ref[rows, cols] = result[i * half:(i + 1) * half]
        done = pl.ds(pl.multiple_of(step * stack * HD, HD), stack * HD)
        pltpu.make_async_copy(attn_ref.at[:, done], attn_hbm.at[:, done], attn_sem.at[step]).start()
        return carry

    steps = KVH * group // stack
    lax.fori_loop(0, steps, attend, 0)

    def finish(step, carry):
        done = pl.ds(pl.multiple_of(step * stack * HD, HD), stack * HD)
        pltpu.make_async_copy(attn_ref.at[:, done], attn_hbm.at[:, done], attn_sem.at[step]).wait()
        return carry

    lax.fori_loop(0, steps, finish, 0)
    own_copy.wait()
    others = pl.ds(0, n - 1)
    pltpu.make_async_copy(pout_ref.at[others], pout_ref.at[others], psend).wait()
    placed = pl.ds(0, (n - 1) * slots)
    pltpu.make_async_copy(outbox_ref.at[placed], outbox_ref.at[placed], isend).wait()
    pltpu.make_async_copy(inbox_hbm.at[placed], inbox_hbm.at[placed], irecv).wait()


def on_device(n, queries, new_kv, prefix_store, page_owner, page_slot, prefix_pages, decode_dest):
    tokens, width = queries.shape
    kv_width = new_kv.shape[1]
    slots = max(1, -(-decode_dest.shape[1] // n))
    prefix = n * PAGE
    bf16 = jnp.bfloat16
    hbm = pl.BlockSpec(memory_space=pl.ANY)
    vmem = pl.BlockSpec(memory_space=pltpu.VMEM)
    return pl.pallas_call(
        functools.partial(kernel, n, slots),
        out_shape=(
            jax.ShapeDtypeStruct((tokens, width), bf16),
            jax.ShapeDtypeStruct((n * slots, PAGE, kv_width), bf16),
        ),
        in_specs=[hbm, hbm, hbm, vmem, vmem, vmem, vmem],
        out_specs=(hbm, hbm),
        scratch_shapes=[
            pltpu.VMEM((tokens, width), bf16),
            pltpu.VMEM((prefix + tokens, kv_width), bf16),
            pltpu.VMEM(prefix_store.shape, bf16),
            pltpu.VMEM((n, PAGE, kv_width), bf16),
            pltpu.VMEM((n, PAGE, kv_width), bf16),
            pltpu.VMEM((n * slots, PAGE, kv_width), bf16),
            pltpu.VMEM((prefix + 3 * (tokens // 2), tokens // 2), bf16),
            pltpu.VMEM((tokens, width), bf16),
            pltpu.SemaphoreType.DMA((3,)),
            pltpu.SemaphoreType.DMA((width // HD,)),
            pltpu.SemaphoreType.DMA,
            pltpu.SemaphoreType.DMA,
            pltpu.SemaphoreType.DMA,
            pltpu.SemaphoreType.DMA,
            pltpu.SemaphoreType.DMA,
        ],
        compiler_params=pltpu.CompilerParams(
            collective_id=0, has_side_effects=True, vmem_limit_bytes=48 * 1024 * 1024
        ),
    )(queries, new_kv, prefix_store, page_owner, page_slot, prefix_pages.reshape(1, n), decode_dest)


def solution(mesh):
    return jax.shard_map(
        functools.partial(on_device, mesh.shape["pool"]),
        mesh=mesh,
        in_specs=(
            P(("groups", "pool"), None),
            P(("groups", "pool"), None),
            P(("groups", "pool"), None, None),
            P("groups", None),
            P("groups", None),
            P("groups"),
            P(("groups", "pool"), None),
        ),
        out_specs=(P(("groups", "pool"), None), P(("groups", "pool"), None, None)),
        check_vma=False,
    )
```

```python
import functools
import math

import jax
import jax.numpy as jnp
from jax import lax
from jax.experimental import pallas as pl
from jax.experimental.pallas import tpu as pltpu
from jax.sharding import PartitionSpec as P

HD = 128
PAGE = 8
KVH = 4
MASKED = -1e30
CHUNKS = 4
VMEM_BYTES = 64 * 1024 * 1024
MESH = pl.DeviceIdType.MESH


def dot(a, b):
    return jnp.dot(a, b, preferred_element_type=jnp.float32)


def dot_t(a, b):
    return lax.dot_general(a, b, (((1,), (1,)), ((), ())), preferred_element_type=jnp.float32)


def iota(shape, dim):
    return lax.broadcasted_iota(jnp.int32, shape, dim)


def kernel(
    n, slots,
    q_hbm, kv_hbm, store_hbm, owner_hbm, slot_hbm, pages_hbm, dest_hbm,
    attn_hbm, inbox_hbm,
    attn_ref, q_ref, keys_ref, store_ref, owner_ref, slot_ref, pages_ref, dest_ref,
    pout_ref, arrived_ref, outbox_ref, bias_ref,
    in_sem, attn_sem, own_sem, psend, precv, isend, irecv,
):
    me = lax.axis_index("pool")
    tokens, width = q_ref.shape
    prefix = n * PAGE
    half = tokens // 2
    group = width // HD // KVH
    new_pages = dest_ref.shape[1]
    kv_width = keys_ref.shape[1]

    load_store = pltpu.make_async_copy(store_hbm, store_ref, in_sem.at[0])
    load_kv = pltpu.make_async_copy(kv_hbm, keys_ref.at[pl.ds(prefix, tokens)], in_sem.at[1])
    load_q = pltpu.make_async_copy(q_hbm, q_ref, in_sem.at[2])
    tables = [
        pltpu.make_async_copy(src, dst, in_sem.at[3 + i])
        for i, (src, dst) in enumerate(
            [(owner_hbm, owner_ref), (slot_hbm, slot_ref), (pages_hbm, pages_ref), (dest_hbm, dest_ref)]
        )
    ]
    for load in tables:
        load.start()
    load_store.start()
    load_kv.start()
    load_q.start()

    def partner(i):
        step = n // 2 + ((i + 1) // 2) * (1 - 2 * (i % 2))
        return (me + step) % n

    barrier = pltpu.get_barrier_semaphore()

    def greet(i, carry):
        pl.semaphore_signal(barrier, inc=1, device_id={"pool": partner(i)}, device_id_type=MESH)
        return carry

    lax.fori_loop(0, n - 1, greet, 0)

    for load in tables:
        load.wait()

    owner = owner_ref[...]
    pages_row = jnp.broadcast_to(pages_ref[...], (n, n))
    row_id, col_id = iota((n, n), 0), iota((n, n), 1)
    pages_col = jnp.sum(jnp.where(row_id == col_id, pages_row, 0), axis=1, keepdims=True)
    wanted = (owner == me) & (col_id < pages_col)
    slot_of = jnp.sum(jnp.where(wanted, slot_ref[...] + 1, 0), axis=1, keepdims=True) - 1
    expand = (iota((prefix, n), 0) // PAGE == iota((prefix, n), 1)).astype(jnp.bfloat16)
    slot_tok = dot(expand, jnp.broadcast_to(slot_of, (n, HD)).astype(jnp.float32).astype(jnp.bfloat16))
    stored_rows = store_ref.shape[0] * PAGE
    row_of = slot_tok.astype(jnp.int32) * PAGE + iota((prefix, HD), 0) % PAGE
    pick = jnp.concatenate(
        [(row_of == iota((prefix, HD), 1) + b).astype(jnp.float32).astype(jnp.bfloat16) for b in range(0, stored_rows, HD)],
        axis=1,
    )
    load_store.wait()
    stored = store_ref[...].astype(jnp.float32).reshape(stored_rows, kv_width).astype(jnp.bfloat16)
    pout_ref[...] = dot(pick, stored).reshape(n, PAGE, kv_width).astype(jnp.bfloat16)

    pl.semaphore_wait(barrier, n - 1)

    def send_page(i, carry):
        to = partner(i)
        pltpu.make_async_remote_copy(
            pout_ref.at[to], arrived_ref.at[me], psend, precv, device_id={"pool": to}, device_id_type=MESH
        ).start()
        return carry

    lax.fori_loop(0, n - 1, send_page, 0)

    dest = jnp.broadcast_to(dest_ref[...], (new_pages, new_pages))
    first, second = iota(dest.shape, 0), iota(dest.shape, 1)
    dest_col = jnp.sum(jnp.where(first == second, dest, 0), axis=1, keepdims=True)
    rank = jnp.sum(jnp.where((dest_col == dest) & (first < second), 1, 0), axis=0, keepdims=True)
    place = (dest_ref[...] * slots + rank).astype(jnp.float32)
    widen = (iota((new_pages, tokens), 1) // PAGE == iota((new_pages, tokens), 0)).astype(jnp.bfloat16)
    place_tok = dot(jnp.broadcast_to(place, (PAGE, new_pages)).astype(jnp.bfloat16), widen)[:1].astype(jnp.int32)
    out_rows = n * slots * PAGE
    goal = place_tok * PAGE + iota((1, tokens), 1) % PAGE
    permute = (iota((out_rows, tokens), 0) == goal).astype(jnp.float32).astype(jnp.bfloat16)
    load_kv.wait()
    new_rows = keys_ref[pl.ds(prefix, tokens), :]
    outbox_ref[...] = dot(permute, new_rows).reshape(n * slots, PAGE, kv_width).astype(jnp.bfloat16)

    def send_new(i, carry):
        to = partner(i)
        pltpu.make_async_remote_copy(
            outbox_ref.at[pl.ds(to * slots, slots)],
            inbox_hbm.at[pl.ds(me * slots, slots)],
            isend, irecv, device_id={"pool": to}, device_id_type=MESH,
        ).start()
        return carry

    lax.fori_loop(0, n - 1, send_new, 0)
    own_copy = pltpu.make_async_copy(
        outbox_ref.at[pl.ds(me * slots, slots)], inbox_hbm.at[pl.ds(me * slots, slots)], own_sem
    )
    own_copy.start()
    arrived_ref[me] = pout_ref[me]

    my_owner = owner_ref[pl.ds(me, 1), :]
    lane = iota((1, n), 1)
    my_pages = jnp.sum(jnp.where(lane == me, pages_ref[...], 0), axis=1, keepdims=True)
    held = jnp.broadcast_to(jnp.where(lane < my_pages, my_owner, -1), (n, n)) == row_id
    valid = jnp.sum(jnp.where(held, 1.0, 0.0), axis=1, keepdims=True)
    valid_tok = dot(expand, jnp.broadcast_to(valid, (n, half)).astype(jnp.bfloat16))
    bias_ref[pl.ds(0, prefix), :] = jnp.where(valid_tok > 0.5, 0.0, MASKED).astype(jnp.bfloat16)
    diagonal = jnp.where(iota((half, half), 0) > iota((half, half), 1), MASKED, 0.0).astype(jnp.bfloat16)
    bias_ref[pl.ds(prefix, half), :] = diagonal
    bias_ref[pl.ds(prefix + half, half), :] = jnp.zeros((half, half), jnp.bfloat16)
    bias_ref[pl.ds(prefix + 2 * half, half), :] = diagonal

    load_q.wait()
    pltpu.make_async_copy(
        arrived_ref.at[pl.ds(0, n - 1)], arrived_ref.at[pl.ds(0, n - 1)], precv
    ).wait()
    keys_ref[pl.ds(0, prefix), :] = (
        arrived_ref[...].astype(jnp.float32).reshape(prefix, kv_width).astype(jnp.bfloat16)
    )

    stack = group if prefix <= 256 else 1
    scale = math.log2(math.e) / math.sqrt(HD)
    unit = (iota((half, half), 0) == iota((half, half), 1)).astype(jnp.float32).astype(jnp.bfloat16)

    def deliver(step):
        done = pl.ds(pl.multiple_of(step * stack * HD, HD), stack * HD)
        return pltpu.make_async_copy(attn_ref.at[:, done], attn_hbm.at[:, done], attn_sem.at[step])

    def attend(step, carry):
        kv_head = step * stack // group
        key_cols = pl.ds(pl.multiple_of(kv_head * HD, HD), HD)
        value_cols = pl.ds(pl.multiple_of(kv_head * HD + KVH * HD, HD), HD)
        heads = [pl.ds(pl.multiple_of((step * stack + i) * HD, HD), HD) for i in range(stack)]
        for part in range(2):
            rows = pl.ds(part * half, half)
            count = prefix + (part + 1) * half
            keys = keys_ref[pl.ds(0, count), key_cols]
            values = keys_ref[pl.ds(0, count), value_cols]
            bias = bias_ref[pl.ds(0, count), :] if part == 0 else jnp.concatenate(
                [bias_ref[pl.ds(0, prefix), :], bias_ref[pl.ds(prefix + half, 2 * half), :]], axis=0
            )
            keyed = jnp.concatenate([keys, bias], axis=1)
            summed = jnp.concatenate([values, jnp.ones((count, HD), jnp.bfloat16)], axis=1)
            query = jnp.concatenate(
                [jnp.concatenate([q_ref[rows, cols], unit], axis=1) for cols in heads], axis=0
            )
            scores = dot_t(query, keyed)
            top = jnp.max(scores, axis=1, keepdims=True)
            weights = jnp.exp2((scores - top) * scale).astype(jnp.bfloat16)
            mixed = dot(weights, summed)
            result = (mixed[:, :HD] / mixed[:, HD:]).astype(jnp.bfloat16)
            for i, cols in enumerate(heads):
                attn_ref[rows, cols] = result[i * half:(i + 1) * half]
        deliver(step).start()
        return carry

    steps = KVH * group // stack
    lax.fori_loop(0, steps, attend, 0)

    def finish(step, carry):
        deliver(step).wait()
        return carry

    lax.fori_loop(0, steps, finish, 0)
    own_copy.wait()
    others = pl.ds(0, n - 1)
    pltpu.make_async_copy(pout_ref.at[others], pout_ref.at[others], psend).wait()
    placed = pl.ds(0, (n - 1) * slots)
    pltpu.make_async_copy(outbox_ref.at[placed], outbox_ref.at[placed], isend).wait()
    pltpu.make_async_copy(inbox_hbm.at[placed], inbox_hbm.at[placed], irecv).wait()


def hand_out(attn_in, inbox_in, attn_out, inbox_out, attn_ref, inbox_ref, sem):
    into, out = [], []
    for a, (source, held, target) in enumerate([(attn_in, attn_ref, attn_out), (inbox_in, inbox_ref, inbox_out)]):
        rows = source.shape[0] // CHUNKS
        for i in range(CHUNKS):
            block = pl.ds(i * rows, rows)
            into.append(pltpu.make_async_copy(source.at[block], held.at[block], sem.at[0, a * CHUNKS + i]))
            out.append(pltpu.make_async_copy(held.at[block], target.at[block], sem.at[1, a * CHUNKS + i]))
    for copy in into:
        copy.start()
    for arrived, leaving in zip(into, out):
        arrived.wait()
        leaving.start()
    for copy in out:
        copy.wait()


def on_device(n, queries, new_kv, prefix_store, page_owner, page_slot, prefix_pages, decode_dest):
    tokens, width = queries.shape
    kv_width = new_kv.shape[1]
    slots = max(1, -(-decode_dest.shape[1] // n))
    prefix = n * PAGE
    bf16 = jnp.bfloat16
    hbm = pl.BlockSpec(memory_space=pltpu.HBM)
    anywhere = pl.BlockSpec(memory_space=pl.ANY)
    vmem = pl.BlockSpec(memory_space=pltpu.VMEM)
    attention, inbox = pl.pallas_call(
        functools.partial(kernel, n, slots),
        out_shape=(
            jax.ShapeDtypeStruct((tokens, width), bf16),
            jax.ShapeDtypeStruct((n * slots, PAGE, kv_width), bf16),
        ),
        in_specs=[hbm] * 7,
        out_specs=(anywhere, anywhere),
        scratch_shapes=[
            pltpu.VMEM((tokens, width), bf16),
            pltpu.VMEM((tokens, width), bf16),
            pltpu.VMEM((prefix + tokens, kv_width), bf16),
            pltpu.VMEM(prefix_store.shape, bf16),
            pltpu.VMEM(page_owner.shape, jnp.int32),
            pltpu.VMEM(page_slot.shape, jnp.int32),
            pltpu.VMEM((1, n), jnp.int32),
            pltpu.VMEM(decode_dest.shape, jnp.int32),
            pltpu.VMEM((n, PAGE, kv_width), bf16),
            pltpu.VMEM((n, PAGE, kv_width), bf16),
            pltpu.VMEM((n * slots, PAGE, kv_width), bf16),
            pltpu.VMEM((prefix + 3 * (tokens // 2), tokens // 2), bf16),
            pltpu.SemaphoreType.DMA((7,)),
            pltpu.SemaphoreType.DMA((width // HD,)),
            pltpu.SemaphoreType.DMA,
            pltpu.SemaphoreType.DMA,
            pltpu.SemaphoreType.DMA,
            pltpu.SemaphoreType.DMA,
            pltpu.SemaphoreType.DMA,
        ],
        compiler_params=pltpu.CompilerParams(
            collective_id=0, has_side_effects=True, vmem_limit_bytes=VMEM_BYTES
        ),
    )(queries, new_kv, prefix_store, page_owner, page_slot, prefix_pages.reshape(1, n), decode_dest)
    return pl.pallas_call(
        hand_out,
        out_shape=(
            jax.ShapeDtypeStruct(attention.shape, bf16),
            jax.ShapeDtypeStruct(inbox.shape, bf16),
        ),
        in_specs=[hbm] * 2,
        out_specs=(hbm, hbm),
        scratch_shapes=[
            pltpu.VMEM(attention.shape, bf16),
            pltpu.VMEM(inbox.shape, bf16),
            pltpu.SemaphoreType.DMA((2, 2 * CHUNKS)),
        ],
        compiler_params=pltpu.CompilerParams(vmem_limit_bytes=VMEM_BYTES),
    )(attention, inbox)


def solution(mesh):
    return jax.shard_map(
        functools.partial(on_device, mesh.shape["pool"]),
        mesh=mesh,
        in_specs=(
            P(("groups", "pool"), None),
            P(("groups", "pool"), None),
            P(("groups", "pool"), None, None),
            P("groups", None),
            P("groups", None),
            P("groups"),
            P(("groups", "pool"), None),
        ),
        out_specs=(P(("groups", "pool"), None), P(("groups", "pool"), None, None)),
        check_vma=False,
    )
```

```python
import functools
import math

import jax
import jax.numpy as jnp
from jax import lax
from jax.experimental import pallas as pl
from jax.experimental.pallas import tpu as pltpu
from jax.sharding import PartitionSpec as P

HD = 128
PAGE = 8
KVH = 4
MASKED = -1e30
CHUNKS = 4
VMEM_BYTES = 48 * 1024 * 1024
MESH = pl.DeviceIdType.MESH


def dot(a, b):
    return jnp.dot(a, b, preferred_element_type=jnp.float32)


def dot_t(a, b):
    return lax.dot_general(a, b, (((1,), (1,)), ((), ())), preferred_element_type=jnp.float32)


def iota(shape, dim):
    return lax.broadcasted_iota(jnp.int32, shape, dim)


def kernel(
    n, slots,
    q_hbm, kv_hbm, store_hbm, owner_hbm, slot_hbm, pages_hbm, dest_hbm,
    attn_ref, inbox_hbm,
    q_ref, keys_ref, store_ref, owner_ref, slot_ref, pages_ref, dest_ref,
    pout_ref, arrived_ref, outbox_ref, bias_ref,
    in_sem, own_sem, psend, precv, isend, irecv,
):
    me = lax.axis_index("pool")
    tokens, width = q_ref.shape
    prefix = n * PAGE
    half = tokens // 2
    group = width // HD // KVH
    new_pages = dest_ref.shape[1]
    kv_width = keys_ref.shape[1]

    load_store = pltpu.make_async_copy(store_hbm, store_ref, in_sem.at[0])
    load_kv = pltpu.make_async_copy(kv_hbm, keys_ref.at[pl.ds(prefix, tokens)], in_sem.at[1])
    load_q = pltpu.make_async_copy(q_hbm, q_ref, in_sem.at[2])
    tables = [
        pltpu.make_async_copy(src, dst, in_sem.at[3 + i])
        for i, (src, dst) in enumerate(
            [(owner_hbm, owner_ref), (slot_hbm, slot_ref), (pages_hbm, pages_ref), (dest_hbm, dest_ref)]
        )
    ]
    for load in tables:
        load.start()
    load_store.start()
    load_kv.start()
    load_q.start()

    def partner(i):
        step = n // 2 + ((i + 1) // 2) * (1 - 2 * (i % 2))
        return (me + step) % n

    barrier = pltpu.get_barrier_semaphore()

    def greet(i, carry):
        pl.semaphore_signal(barrier, inc=1, device_id={"pool": partner(i)}, device_id_type=MESH)
        return carry

    lax.fori_loop(0, n - 1, greet, 0)

    for load in tables:
        load.wait()

    owner = owner_ref[...]
    pages_row = jnp.broadcast_to(pages_ref[...], (n, n))
    row_id, col_id = iota((n, n), 0), iota((n, n), 1)
    pages_col = jnp.sum(jnp.where(row_id == col_id, pages_row, 0), axis=1, keepdims=True)
    wanted = (owner == me) & (col_id < pages_col)
    slot_of = jnp.sum(jnp.where(wanted, slot_ref[...] + 1, 0), axis=1, keepdims=True) - 1
    expand = (iota((prefix, n), 0) // PAGE == iota((prefix, n), 1)).astype(jnp.bfloat16)
    slot_tok = dot(expand, jnp.broadcast_to(slot_of, (n, HD)).astype(jnp.float32).astype(jnp.bfloat16))
    stored_rows = store_ref.shape[0] * PAGE
    row_of = slot_tok.astype(jnp.int32) * PAGE + iota((prefix, HD), 0) % PAGE
    pick = jnp.concatenate(
        [(row_of == iota((prefix, HD), 1) + b).astype(jnp.float32).astype(jnp.bfloat16) for b in range(0, stored_rows, HD)],
        axis=1,
    )
    load_store.wait()
    stored = store_ref[...].astype(jnp.float32).reshape(stored_rows, kv_width).astype(jnp.bfloat16)
    pout_ref[...] = dot(pick, stored).reshape(n, PAGE, kv_width).astype(jnp.bfloat16)

    pl.semaphore_wait(barrier, n - 1)

    def send_page(i, carry):
        to = partner(i)
        pltpu.make_async_remote_copy(
            pout_ref.at[to], arrived_ref.at[me], psend, precv, device_id={"pool": to}, device_id_type=MESH
        ).start()
        return carry

    lax.fori_loop(0, n - 1, send_page, 0)

    dest = jnp.broadcast_to(dest_ref[...], (new_pages, new_pages))
    first, second = iota(dest.shape, 0), iota(dest.shape, 1)
    dest_col = jnp.sum(jnp.where(first == second, dest, 0), axis=1, keepdims=True)
    rank = jnp.sum(jnp.where((dest_col == dest) & (first < second), 1, 0), axis=0, keepdims=True)
    place = (dest_ref[...] * slots + rank).astype(jnp.float32)
    widen = (iota((new_pages, tokens), 1) // PAGE == iota((new_pages, tokens), 0)).astype(jnp.bfloat16)
    place_tok = dot(jnp.broadcast_to(place, (PAGE, new_pages)).astype(jnp.bfloat16), widen)[:1].astype(jnp.int32)
    out_rows = n * slots * PAGE
    goal = place_tok * PAGE + iota((1, tokens), 1) % PAGE
    permute = (iota((out_rows, tokens), 0) == goal).astype(jnp.float32).astype(jnp.bfloat16)
    load_kv.wait()
    new_rows = keys_ref[pl.ds(prefix, tokens), :]
    outbox_ref[...] = dot(permute, new_rows).reshape(n * slots, PAGE, kv_width).astype(jnp.bfloat16)

    def send_new(i, carry):
        to = partner(i)
        pltpu.make_async_remote_copy(
            outbox_ref.at[pl.ds(to * slots, slots)],
            inbox_hbm.at[pl.ds(me * slots, slots)],
            isend, irecv, device_id={"pool": to}, device_id_type=MESH,
        ).start()
        return carry

    lax.fori_loop(0, n - 1, send_new, 0)
    own_copy = pltpu.make_async_copy(
        outbox_ref.at[pl.ds(me * slots, slots)], inbox_hbm.at[pl.ds(me * slots, slots)], own_sem
    )
    own_copy.start()
    arrived_ref[me] = pout_ref[me]

    my_owner = owner_ref[pl.ds(me, 1), :]
    lane = iota((1, n), 1)
    my_pages = jnp.sum(jnp.where(lane == me, pages_ref[...], 0), axis=1, keepdims=True)
    held = jnp.broadcast_to(jnp.where(lane < my_pages, my_owner, -1), (n, n)) == row_id
    valid = jnp.sum(jnp.where(held, 1.0, 0.0), axis=1, keepdims=True)
    valid_tok = dot(expand, jnp.broadcast_to(valid, (n, half)).astype(jnp.bfloat16))
    bias_ref[pl.ds(0, prefix), :] = jnp.where(valid_tok > 0.5, 0.0, MASKED).astype(jnp.bfloat16)
    diagonal = jnp.where(iota((half, half), 0) > iota((half, half), 1), MASKED, 0.0).astype(jnp.bfloat16)
    bias_ref[pl.ds(prefix, half), :] = diagonal
    bias_ref[pl.ds(prefix + half, half), :] = jnp.zeros((half, half), jnp.bfloat16)
    bias_ref[pl.ds(prefix + 2 * half, half), :] = diagonal

    load_q.wait()
    pltpu.make_async_copy(
        arrived_ref.at[pl.ds(0, n - 1)], arrived_ref.at[pl.ds(0, n - 1)], precv
    ).wait()
    keys_ref[pl.ds(0, prefix), :] = (
        arrived_ref[...].astype(jnp.float32).reshape(prefix, kv_width).astype(jnp.bfloat16)
    )

    stack = group if prefix <= 256 else 1
    scale = math.log2(math.e) / math.sqrt(HD)
    unit = (iota((half, half), 0) == iota((half, half), 1)).astype(jnp.float32).astype(jnp.bfloat16)

    def attend(step, carry):
        kv_head = step * stack // group
        key_cols = pl.ds(pl.multiple_of(kv_head * HD, HD), HD)
        value_cols = pl.ds(pl.multiple_of(kv_head * HD + KVH * HD, HD), HD)
        heads = [pl.ds(pl.multiple_of((step * stack + i) * HD, HD), HD) for i in range(stack)]
        for part in range(2):
            rows = pl.ds(part * half, half)
            count = prefix + (part + 1) * half
            keys = keys_ref[pl.ds(0, count), key_cols]
            values = keys_ref[pl.ds(0, count), value_cols]
            bias = bias_ref[pl.ds(0, count), :] if part == 0 else jnp.concatenate(
                [bias_ref[pl.ds(0, prefix), :], bias_ref[pl.ds(prefix + half, 2 * half), :]], axis=0
            )
            keyed = jnp.concatenate([keys, bias], axis=1)
            summed = jnp.concatenate([values, jnp.ones((count, HD), jnp.bfloat16)], axis=1)
            query = jnp.concatenate(
                [jnp.concatenate([q_ref[rows, cols], unit], axis=1) for cols in heads], axis=0
            )
            scores = dot_t(query, keyed)
            top = jnp.max(scores, axis=1, keepdims=True)
            weights = jnp.exp2((scores - top) * scale).astype(jnp.bfloat16)
            mixed = dot(weights, summed)
            result = (mixed[:, :HD] / mixed[:, HD:]).astype(jnp.bfloat16)
            for i, cols in enumerate(heads):
                attn_ref[rows, cols] = result[i * half:(i + 1) * half]
        return carry

    steps = KVH * group // stack
    lax.fori_loop(0, steps, attend, 0)

    own_copy.wait()
    others = pl.ds(0, n - 1)
    pltpu.make_async_copy(pout_ref.at[others], pout_ref.at[others], psend).wait()
    placed = pl.ds(0, (n - 1) * slots)
    pltpu.make_async_copy(outbox_ref.at[placed], outbox_ref.at[placed], isend).wait()
    pltpu.make_async_copy(inbox_hbm.at[placed], inbox_hbm.at[placed], irecv).wait()


def hand_out(attn_ref, inbox_ref, attn_hbm, inbox_hbm, sem):
    rows = attn_ref.shape[0] // CHUNKS
    copies = [
        pltpu.make_async_copy(attn_ref.at[pl.ds(i * rows, rows)], attn_hbm.at[pl.ds(i * rows, rows)], sem.at[i])
        for i in range(CHUNKS)
    ] + [pltpu.make_async_copy(inbox_ref, inbox_hbm, sem.at[CHUNKS])]
    for copy in copies:
        copy.start()
    for copy in copies:
        copy.wait()


def on_device(n, queries, new_kv, prefix_store, page_owner, page_slot, prefix_pages, decode_dest):
    tokens, width = queries.shape
    kv_width = new_kv.shape[1]
    slots = max(1, -(-decode_dest.shape[1] // n))
    prefix = n * PAGE
    bf16 = jnp.bfloat16
    hbm = pl.BlockSpec(memory_space=pltpu.HBM)
    vmem = pl.BlockSpec(memory_space=pltpu.VMEM)
    attention, inbox = pl.pallas_call(
        functools.partial(kernel, n, slots),
        out_shape=(
            pltpu.VMEM((tokens, width), bf16),
            pltpu.VMEM((n * slots, PAGE, kv_width), bf16),
        ),
        in_specs=[hbm] * 7,
        out_specs=(vmem, vmem),
        scratch_shapes=[
            pltpu.VMEM((tokens, width), bf16),
            pltpu.VMEM((prefix + tokens, kv_width), bf16),
            pltpu.VMEM(prefix_store.shape, bf16),
            pltpu.VMEM(page_owner.shape, jnp.int32),
            pltpu.VMEM(page_slot.shape, jnp.int32),
            pltpu.VMEM((1, n), jnp.int32),
            pltpu.VMEM(decode_dest.shape, jnp.int32),
            pltpu.VMEM((n, PAGE, kv_width), bf16),
            pltpu.VMEM((n, PAGE, kv_width), bf16),
            pltpu.VMEM((n * slots, PAGE, kv_width), bf16),
            pltpu.VMEM((prefix + 3 * (tokens // 2), tokens // 2), bf16),
            pltpu.SemaphoreType.DMA((7,)),
            pltpu.SemaphoreType.DMA,
            pltpu.SemaphoreType.DMA,
            pltpu.SemaphoreType.DMA,
            pltpu.SemaphoreType.DMA,
            pltpu.SemaphoreType.DMA,
        ],
        compiler_params=pltpu.CompilerParams(
            collective_id=0, has_side_effects=True, vmem_limit_bytes=VMEM_BYTES
        ),
    )(*[
        pltpu.with_memory_space_constraint(x, pltpu.HBM)
        for x in (queries, new_kv, prefix_store, page_owner, page_slot, prefix_pages.reshape(1, n), decode_dest)
    ])
    return pl.pallas_call(
        hand_out,
        out_shape=(
            jax.ShapeDtypeStruct(attention.shape, bf16),
            jax.ShapeDtypeStruct(inbox.shape, bf16),
        ),
        in_specs=[vmem] * 2,
        out_specs=(hbm, hbm),
        scratch_shapes=[pltpu.SemaphoreType.DMA((CHUNKS + 1,))],
    )(*[pltpu.with_memory_space_constraint(x, pltpu.VMEM) for x in (attention, inbox)])


def solution(mesh):
    return jax.shard_map(
        functools.partial(on_device, mesh.shape["pool"]),
        mesh=mesh,
        in_specs=(
            P(("groups", "pool"), None),
            P(("groups", "pool"), None),
            P(("groups", "pool"), None, None),
            P("groups", None),
            P("groups", None),
            P("groups"),
            P(("groups", "pool"), None),
        ),
        out_specs=(P(("groups", "pool"), None), P(("groups", "pool"), None, None)),
        check_vma=False,
    )
```
